256 devices in a mesh: seq: 32 (over z, y_lo, core), fsdp: 8 (over y_hi, x).
Axes of the slice: x: 4, y: 4 (y_hi: 2, y_lo: 2; y = y_hi * 2 + y_lo), z: 8, core: 2. Of those that a mesh axis runs over, the one named last changes fastest.
Arguments:
- queries: bfloat16 [16, 2048, 4096], P('fsdp', 'seq'), may hold values from -6 to 6
- key_rows: bfloat16 [16, 2048, 4096], P('fsdp', 'seq'), may hold values from -6 to 6
- value_rows: bfloat16 [16, 2048, 4096], P('fsdp', 'seq'), may hold values from -6 to 6
- query_tan: bfloat16 [16, 2048, 4096], P('fsdp', 'seq'), may hold values from -6 to 6
- key_tan: bfloat16 [16, 2048, 4096], P('fsdp', 'seq'), may hold values from -6 to 6
- value_tan: bfloat16 [16, 2048, 4096], P('fsdp', 'seq'), may hold values from -6 to 6
- residual: bfloat16 [16, 2048, 2560], P('fsdp', 'seq'), may hold values from -4 to 4
- residual_tan: bfloat16 [16, 2048, 2560], P('fsdp', 'seq'), may hold values from -6 to 6
- cond_mask: int32 [16, 2048], P('fsdp', 'seq'), may hold values 0 or 1
- time_index: int32 [16], P('fsdp'), may hold values from 0 to 63
- gate_table: float32 [64, 2560], replicated, may hold values from 0.5 to 1.5
- gate_slope: float32 [64, 2560], replicated, may hold values from -1 to 1
- out_weight: bfloat16 [4096, 2560], P(('seq', 'fsdp')), may hold values from -0.75 to 0.75
Outputs:
- block_out: bfloat16 [16, 2048, 2560], P('fsdp', 'seq')
- block_tan: bfloat16 [16, 2048, 2560], P('fsdp', 'seq')
The draws below stay inside these ranges and needn't reach their ends.
All inputs are finite; a program needn't handle non-finite values. No bound on the sum of `cond_mask` on one device may be relied on, other than what follows from the above.
Results may differ from the reference program's by a relative error of at most 0.0057.
Values may be sent and summed in bfloat16 or wider, within the bound.
A program may use at most 128 MiB of HBM per device.

```python
import math
import jax
import jax.numpy as jnp
from jax import lax

HEADS = 32
HEAD_DIM = 128
OUT_WIDTH = 2560
STEPS = 64
SEQ_LEN = 2048
CLIPS = 16


def field_draw(key, planted):
    key = jax.random.fold_in(key, 101)
    shape = (CLIPS, SEQ_LEN, HEADS * HEAD_DIM)
    key_one = jax.random.fold_in(key, 0)
    key_three = jax.random.fold_in(key, 2)
    key_four = jax.random.fold_in(key, 3)
    gauss = jnp.clip(jax.random.normal(key_one, shape, jnp.float32), -6.0, 6.0)
    field = gauss
    for planted_row in range(planted):
        target = planted_row * SEQ_LEN // 4 + SEQ_LEN // 8 + 2
        magnitude = jax.random.uniform(jax.random.fold_in(key_three, planted_row), (CLIPS, HEADS * HEAD_DIM), jnp.float32, 0.9, 1.0)
        coin = jax.random.bernoulli(jax.random.fold_in(key_four, planted_row), 0.5, (CLIPS, HEADS * HEAD_DIM))
        row_values = 6.0 * magnitude * jnp.where(coin, 1.0, -1.0)
        strength = (planted_row + 1) / planted
        per_head = row_values.reshape(CLIPS, HEADS, HEAD_DIM)
        peak_score = strength * jnp.sum(per_head * per_head, -1, keepdims=True) / math.sqrt(HEAD_DIM)
        second = (per_head * (1.0 - 2.0 / peak_score)).reshape(CLIPS, HEADS * HEAD_DIM)
        field = field.at[:, target].set(row_values).at[:, target + 1].set(second)
    return field


def draw_key_rows(key, part):
    field = field_draw(key, 0)
    return field.astype(jnp.bfloat16)


def draw_queries(key, part):
    planted = 0
    shared = field_draw(key, planted)
    key = jax.random.fold_in(key, 3)
    shape = (CLIPS, SEQ_LEN, HEADS * HEAD_DIM)
    key_one = jax.random.fold_in(key, 0)
    gauss = jnp.clip(jax.random.normal(key_one, shape, jnp.float32), -6.0, 6.0)
    field = gauss
    for planted_row in range(planted):
        target = planted_row * SEQ_LEN // 4 + SEQ_LEN // 8 + 2
        source = planted_row * SEQ_LEN // 4 + 1
        strength = (planted_row + 1) / planted
        field = field.at[:, source].set(strength * shared[:, target])
    return field.astype(jnp.bfloat16)


def set_ends(values, rng, least, largest):
    place = [jax.random.randint(jax.random.fold_in(rng, axis), (), 0, length) for axis, length in enumerate(values.shape)]
    longest = values.shape.index(max(values.shape))
    beside = place[:longest] + [(place[longest] + 1) % values.shape[longest]] + place[longest + 1:]
    return values.at[tuple(place)].set(least).at[tuple(beside)].set(largest)


def block_levels(key, extent, shards, low, high):
    loudness = 1.0
    for axis_at, shards_of in shards:
        draws = jax.random.uniform(jax.random.fold_in(jax.random.fold_in(key, 6), axis_at), (shards_of,), jnp.float32, low / len(shards), high / len(shards))
        loudness = loudness * jnp.repeat(jnp.exp(draws), extent[axis_at] // shards_of).reshape((-1,) + (1,) * (len(extent) - 1 - axis_at))
    return loudness


def scatter_about(stream_key, shape, scale, reach, pieces=(), kind=jnp.bfloat16):
    values = scale * jax.random.normal(stream_key, shape, jnp.float32)
    if pieces:
        values = values * block_levels(stream_key, shape, pieces, -0.22, 0.18)
    return jnp.clip(values, -reach, reach).astype(kind)


def setup_inputs(seed: int = 0) -> dict:
    streams_of = jax.random.split(jax.random.key(seed), 14)
    return {
        "queries": draw_queries(jax.random.fold_in(streams_of[13], 71), 0),
        "key_rows": draw_key_rows(jax.random.fold_in(streams_of[13], 71), 0),
        "value_rows": scatter_about(streams_of[2], (CLIPS, SEQ_LEN, HEADS * HEAD_DIM), 1.0, 6.0, ((0, 8), (1, 32))),
        "query_tan": scatter_about(streams_of[3], (CLIPS, SEQ_LEN, HEADS * HEAD_DIM), 1.0, 6.0, ((0, 8), (1, 32))),
        "key_tan": scatter_about(streams_of[4], (CLIPS, SEQ_LEN, HEADS * HEAD_DIM), 1.0, 6.0, ((0, 8), (1, 32))),
        "value_tan": scatter_about(streams_of[5], (CLIPS, SEQ_LEN, HEADS * HEAD_DIM), 1.0, 6.0, ((0, 8), (1, 32))),
        "residual": scatter_about(streams_of[6], (CLIPS, SEQ_LEN, OUT_WIDTH), 0.5, 4.0, ((0, 8), (1, 32))),
        "residual_tan": scatter_about(streams_of[7], (CLIPS, SEQ_LEN, OUT_WIDTH), 1.0, 6.0, ((0, 8), (1, 32))),
        "cond_mask": set_ends((jax.random.randint(streams_of[8], (CLIPS, SEQ_LEN), 0, 3) < 1).astype(jnp.int32), jax.random.fold_in(streams_of[8], 1), 0, 1),
        "time_index": set_ends(jax.random.randint(streams_of[9], (CLIPS,), 0, STEPS), jax.random.fold_in(streams_of[9], 1), 0, STEPS - 1).astype(jnp.int32),
        "gate_table": jnp.clip(jax.random.uniform(streams_of[10], (STEPS, OUT_WIDTH), jnp.float32, 0.5, 1.5), 0.5, 1.5),
        "gate_slope": jnp.clip(jax.random.uniform(streams_of[11], (STEPS, OUT_WIDTH), jnp.float32, -1.0, 1.0), -1.0, 1.0),
        "out_weight": scatter_about(streams_of[12], (HEADS * HEAD_DIM, OUT_WIDTH), (HEADS * HEAD_DIM // 64) ** -0.5, 0.75, ((0, 256),)),
    }


def head_attention(tensors):
    query_head, key_head, value_head, query_dot, key_dot, value_dot = tensors
    length = query_head.shape[0]
    block_rows = math.gcd(length, 512)
    score_scale = HEAD_DIM ** -0.5
    block_pairs = (query_head.reshape(length // block_rows, block_rows, HEAD_DIM),
                   query_dot.reshape(length // block_rows, block_rows, HEAD_DIM))

    def one_block(block_pair):
        query_blk, query_blk_dot = block_pair
        scores = jnp.dot(query_blk, key_head.T, preferred_element_type=jnp.float32) * score_scale
        score_tan = (jnp.dot(query_blk_dot, key_head.T, preferred_element_type=jnp.float32)
                     + jnp.dot(query_blk, key_dot.T, preferred_element_type=jnp.float32)) * score_scale
        row_peak = jnp.max(scores, -1, keepdims=True)
        shifted_exp = jnp.exp(scores - row_peak)
        softmax = shifted_exp / jnp.sum(shifted_exp, -1, keepdims=True)
        softmax_low = softmax.astype(jnp.bfloat16)
        centre = jnp.sum(softmax * score_tan, -1, keepdims=True)
        weight_tan = (softmax * (score_tan - centre)).astype(jnp.bfloat16)
        attended = jnp.dot(softmax_low, value_head, preferred_element_type=jnp.float32)
        attended_tan = (jnp.dot(weight_tan, value_head, preferred_element_type=jnp.float32)
                        + jnp.dot(softmax_low, value_dot, preferred_element_type=jnp.float32))
        return attended.astype(jnp.bfloat16), attended_tan.astype(jnp.bfloat16)

    outputs, tangents = lax.map(one_block, block_pairs)
    return outputs.reshape(length, HEAD_DIM), tangents.reshape(length, HEAD_DIM)


def reference(queries, key_rows, value_rows, query_tan, key_tan, value_tan, residual, residual_tan,
              cond_mask, time_index, gate_table, gate_slope, out_weight):
    live = (cond_mask == 0)[..., None]
    nothing = jnp.zeros((), jnp.bfloat16)
    query_live = jnp.where(live, query_tan, nothing)
    key_live = jnp.where(live, key_tan, nothing)
    value_live = jnp.where(live, value_tan, nothing)

    def heads_first(array):
        return array.reshape(SEQ_LEN, HEADS, HEAD_DIM).transpose(1, 0, 2)

    def per_clip(items):
        (clip_query, clip_key, clip_value, clip_qdot, clip_kdot, clip_vdot,
         clip_resid, clip_rdot, clip_live, clip_time) = items
        outputs, tangents = lax.map(head_attention, (
            heads_first(clip_query), heads_first(clip_key), heads_first(clip_value),
            heads_first(clip_qdot), heads_first(clip_kdot), heads_first(clip_vdot)))
        tokens_out = outputs.transpose(1, 0, 2).reshape(SEQ_LEN, HEADS * HEAD_DIM)
        tokens_tan = tangents.transpose(1, 0, 2).reshape(SEQ_LEN, HEADS * HEAD_DIM)
        projected = jnp.dot(tokens_out, out_weight, preferred_element_type=jnp.float32)
        projected_tan = jnp.dot(tokens_tan, out_weight, preferred_element_type=jnp.float32)
        gate = gate_table[clip_time]
        slope = gate_slope[clip_time]
        block_out = (clip_resid.astype(jnp.float32) + gate * projected).astype(jnp.bfloat16)
        kept_tan = jnp.where(clip_live, clip_rdot, nothing).astype(jnp.float32)
        block_tan = (kept_tan + slope * projected + gate * projected_tan).astype(jnp.bfloat16)
        return block_out, block_tan

    results = lax.map(per_clip, (queries, key_rows, value_rows, query_live, key_live, value_live,
                                 residual, residual_tan, live, time_index))
    return results[0], results[1]
```

```python
import functools
import math

import jax
import jax.numpy as jnp
from jax import lax
from jax.experimental import pallas as pl
from jax.experimental.pallas import tpu as pltpu
from jax.sharding import PartitionSpec as P

HEAD_DIM = 128
Y_LO, CORE, Y_HI = 2, 2, 2
GROUP = Y_LO * CORE
CLIPS = 2
NARROW = jnp.bfloat16
WIDE = jnp.float32


def column_of(row, length):
    square = (length, length)
    same = lax.broadcasted_iota(jnp.int32, square, 0) == lax.broadcasted_iota(jnp.int32, square, 1)
    return jnp.sum(jnp.where(same, jnp.broadcast_to(row, square), 0.0), 1, keepdims=True)


def kernel(
    dims,
    q_ref, k_ref, v_ref, qt_ref, kt_ref, vt_ref, res_ref, rest_ref,
    mask_ref, time_ref, gate_ref, slope_ref, weight_ref,
    out_ref, tan_ref,
    raw, kvsend, kvbuf, qsend, qbuf, osend, orecv, wbuf, resbuf, gatebuf,
    scores, probs, sums, joined,
    load_sem, res_sem, kv_ss, kv_rs, q_ss, q_rs, o_ss, o_rs, w_ss, w_rs, own_sem,
):
    n_z, n_x, tok, n_out = dims
    n_seq = n_z * GROUP
    length = n_seq * tok
    d = HEAD_DIM
    rows = GROUP * tok
    me = lax.axis_index("seq")
    my_f = lax.axis_index("fsdp")
    z, y_lo, core = me // GROUP, (me // CORE) % Y_LO, me % CORE
    y_hi, x = my_f // n_x, my_f % n_x
    y_hi_count = dims_y_hi(dims)

    def seq_peer(slot, sign):
        ring = slot // GROUP
        half = (ring + 1) // 2
        dz = (2 * (ring % 2) - 1) * half * sign
        pz = (z + dz + n_z) % n_z
        py = (y_lo + (slot // CORE) % Y_LO) % Y_LO
        pc = (core + slot) % CORE
        return pz * GROUP + py * CORE + pc

    def device(seq, fsdp):
        return {"seq": seq, "fsdp": fsdp}

    x_peers = [device(me, y_hi * n_x + (x + dx) % n_x) for dx in range(1, n_x)]
    y_peers = [
        device(
            z * GROUP + ((y_lo + a) % Y_LO) * CORE + core,
            ((y_hi + b) % y_hi_count) * n_x + x,
        )
        for b in range(y_hi_count)
        for a in range(Y_LO)
        if (a, b) != (0, 0)
    ]
    y_far = [p for p, (b, a) in zip(
        y_peers,
        [(b, a) for b in range(y_hi_count) for a in range(Y_LO) if (a, b) != (0, 0)],
    ) if b]

    streams = (k_ref, kt_ref, v_ref, vt_ref, qt_ref, q_ref)

    def load(clip, stream):
        return pltpu.make_async_copy(
            streams[stream].at[clip], raw.at[clip, stream], load_sem.at[clip, stream]
        )

    for clip in range(CLIPS):
        for stream in range(6):
            load(clip, stream).start()
    own_weight = pltpu.make_async_copy(weight_ref, wbuf.at[z, y_lo, core, y_hi, x], own_sem.at[0])
    own_weight.start()
    late_loads = [
        pltpu.make_async_copy(res_ref, resbuf.at[0], res_sem.at[0]),
        pltpu.make_async_copy(rest_ref, resbuf.at[1], res_sem.at[1]),
        pltpu.make_async_copy(gate_ref, gatebuf.at[0], res_sem.at[2]),
        pltpu.make_async_copy(slope_ref, gatebuf.at[1], res_sem.at[3]),
    ]

    barrier = pltpu.get_barrier_semaphore()

    def greet(slot, carry):
        pl.semaphore_signal(barrier, inc=1, device_id=device(seq_peer(slot, 1), my_f))
        return carry

    lax.fori_loop(1, n_seq, greet, 0)
    for peer in x_peers + y_far:
        pl.semaphore_signal(barrier, inc=1, device_id=peer)

    live = [
        column_of((mask_ref[pl.ds(clip, 1), :] == 0).astype(WIDE), tok) for clip in range(CLIPS)
    ]

    def pack_kv(clip):
        for stream in range(4):
            load(clip, stream).wait()

        def one(head, carry):
            lanes = pl.ds(pl.multiple_of(head * d, d), d)
            for stream in range(4):
                part = raw[clip, stream, :, lanes]
                if stream % 2:
                    part = (part.astype(WIDE) * live[clip]).astype(NARROW)
                kvsend[clip, head, :, stream * d : (stream + 1) * d] = part
            return carry

        lax.fori_loop(0, n_seq, one, 0)

    def pack_q(clip):
        for stream in range(4, 6):
            load(clip, stream).wait()

        def one(head, carry):
            lanes = pl.ds(pl.multiple_of(head * d, d), d)
            part = raw[clip, 4, :, lanes]
            qsend[clip, head, :, :d] = (part.astype(WIDE) * live[clip]).astype(NARROW)
            qsend[clip, head, :, d:] = raw[clip, 5, :, lanes]
            return carry

        lax.fori_loop(0, n_seq, one, 0)

    def send_kv(clip):
        def one(slot, carry):
            peer = seq_peer(slot, 1)
            pltpu.make_async_remote_copy(
                src_ref=kvsend.at[clip, peer],
                dst_ref=kvbuf.at[clip, pl.ds(pl.multiple_of(slot * tok, tok), tok)],
                send_sem=kv_ss.at[clip],
                recv_sem=kv_rs.at[clip],
                device_id=device(peer, my_f),
            ).start()
            return carry

        lax.fori_loop(1, n_seq, one, 0)
        kvbuf[clip, :tok] = kvsend[clip, me]

    def send_q(clip):
        def one(slot, carry):
            peer = seq_peer(slot, 1)
            pltpu.make_async_remote_copy(
                src_ref=qsend.at[clip, peer],
                dst_ref=qbuf.at[clip, pl.ds(pl.multiple_of(slot * tok, tok), tok)],
                send_sem=q_ss.at[clip],
                recv_sem=q_rs.at[clip, slot // GROUP],
                device_id=device(peer, my_f),
            ).start()
            return carry

        lax.fori_loop(1, n_seq, one, 0)
        qbuf[clip, :tok] = qsend[clip, me]

    def drain(ref, sem):
        pltpu.make_async_copy(ref, ref, sem).wait()

    pack_kv(0)
    pl.semaphore_wait(barrier, n_seq - 1 + len(x_peers) + len(y_far))

    own_weight.wait()
    mine = wbuf.at[z, y_lo, core, y_hi, x]

    def spread_z(step, carry):
        peer_z = (z + step) % n_z
        pltpu.make_async_remote_copy(
            src_ref=mine, dst_ref=mine, send_sem=w_ss.at[0], recv_sem=w_rs.at[0],
            device_id=device(peer_z * GROUP + y_lo * CORE + core, my_f),
        ).start()
        return carry

    lax.fori_loop(1, n_z, spread_z, 0)
    send_kv(0)
    pack_q(0)
    send_q(0)
    pack_kv(1)
    send_kv(1)
    pack_q(1)
    send_q(1)
    for copy in late_loads:
        copy.start()

    drain(wbuf.at[: n_z - 1, 0, 0, 0, 0], w_rs.at[0])
    for peer in y_peers:
        part = wbuf.at[:, y_lo, core, y_hi, x]
        pltpu.make_async_remote_copy(
            src_ref=part, dst_ref=part, send_sem=w_ss.at[1], recv_sem=w_rs.at[1], device_id=peer
        ).start()
    drain(wbuf.at[:, 0, 0, 0, : len(y_peers)], w_rs.at[1])
    for peer in x_peers:
        part = wbuf.at[:, :, core, :, x]
        pltpu.make_async_remote_copy(
            src_ref=part, dst_ref=part, send_sem=w_ss.at[2], recv_sem=w_rs.at[2], device_id=peer
        ).start()

    scale = d ** (-0.5)
    to_exponent = scale * math.log2(math.e)
    step_rows = 16

    def attend(clip):
        drain(kvbuf.at[clip, tok:], kv_rs.at[clip])

        def block(index, carry):
            start = pl.multiple_of(index * rows, rows)

            @pl.when(index == 0)
            def _():
                drain(qbuf.at[clip, tok:rows], q_rs.at[clip, 0])

            @pl.when(index != 0)
            def _():
                drain(qbuf.at[clip, pl.ds(start, rows)], q_rs.at[clip, index])

            both = qbuf[clip, pl.ds(start, rows)]
            plain = both[:, d:]
            left = jnp.concatenate(
                [jnp.concatenate([plain, jnp.zeros_like(plain)], 1), both], 0
            )
            scores[...] = lax.dot_general(
                left, kvbuf[clip, :, : 2 * d], (((1,), (1,)), ((), ())),
                preferred_element_type=WIDE,
            )

            def soften(step, carry):
                at = pl.multiple_of(step * step_rows, step_rows)
                exponent = scores[pl.ds(at, step_rows)] * to_exponent
                weight = jnp.exp2(exponent - jnp.max(exponent, 1, keepdims=True))
                total = jnp.sum(weight, 1, keepdims=True)
                slant = scores[pl.ds(rows + at, step_rows)]
                centre = jnp.sum(weight * slant, 1, keepdims=True) / total
                probs[pl.ds(at, step_rows)] = weight.astype(NARROW)
                probs[pl.ds(rows + at, step_rows)] = (weight * (slant - centre)).astype(NARROW)
                sums[pl.ds(at, step_rows)] = jnp.broadcast_to(1.0 / total, (step_rows, d))
                return carry

            lax.fori_loop(0, rows // step_rows, soften, 0)
            result = jnp.dot(
                probs[...], kvbuf[clip, :, 2 * d :], preferred_element_type=WIDE
            )
            inverse = sums[...]
            value = (result[:rows, :d] * inverse).astype(NARROW)
            value_tan = (
                (result[rows:, :d] * scale + result[:rows, d:]) * inverse
            ).astype(NARROW)
            for part in range(GROUP):
                slot = index * GROUP + part
                at = slice(part * tok, (part + 1) * tok)
                osend[clip, slot, :tok] = value[at]
                osend[clip, slot, tok:] = value_tan[at]
            for part in range(GROUP):
                slot = index * GROUP + part
                copy = pltpu.make_async_remote_copy(
                    src_ref=osend.at[clip, slot],
                    dst_ref=orecv.at[clip, me],
                    send_sem=o_ss.at[clip],
                    recv_sem=o_rs.at[clip],
                    device_id=device(seq_peer(slot, -1), my_f),
                )
                if part:
                    copy.start()
                else:
                    pl.when(index != 0)(copy.start)
            return carry

        lax.fori_loop(0, n_z, block, 0)
        orecv[clip, me] = osend[clip, 0]

    attend(0)
    drain(wbuf.at[:, :, 0, :, : n_x - 1], w_rs.at[2])
    part = wbuf.at[:, :, core]
    pltpu.make_async_remote_copy(
        src_ref=part, dst_ref=part, send_sem=w_ss.at[3], recv_sem=w_rs.at[3],
        device_id=device(z * GROUP + y_lo * CORE + (core + 1) % CORE, my_f),
    ).start()
    attend(1)
    drain(wbuf.at[:, :, 0], w_rs.at[3])
    for copy in late_loads:
        copy.wait()

    tile = 256
    steps = gatebuf.shape[1]

    def project(clip):
        drain(orecv.at[clip, : n_seq - 1], o_rs.at[clip])
        for head in range(n_seq):
            joined[:, head * d : (head + 1) * d] = orecv[clip, head]
        picked = (
            lax.broadcasted_iota(jnp.int32, (steps, 1), 0) == time_ref[clip]
        ).astype(WIDE)

        def one(index, carry):
            lanes = pl.ds(pl.multiple_of(index * tile, tile), tile)
            weight = wbuf[:, :, :, :, :, :, lanes].reshape(n_seq * d, tile)
            both = jnp.dot(joined[...], weight, preferred_element_type=WIDE)
            gate = jnp.sum(gatebuf[0, :, lanes] * picked, 0, keepdims=True)
            slope = jnp.sum(gatebuf[1, :, lanes] * picked, 0, keepdims=True)
            plain, tangent = both[:tok], both[tok:]
            out_ref[clip, :, lanes] = (
                resbuf[0, clip, :, lanes].astype(WIDE) + gate * plain
            ).astype(NARROW)
            tan_ref[clip, :, lanes] = (
                resbuf[1, clip, :, lanes].astype(WIDE) * live[clip] + slope * plain + gate * tangent
            ).astype(NARROW)
            return carry

        lax.fori_loop(0, n_out // tile, one, 0)

    project(0)
    project(1)

    for clip in range(CLIPS):
        drain(kvsend.at[clip, : n_seq - 1], kv_ss.at[clip])
        drain(qsend.at[clip, : n_seq - 1], q_ss.at[clip])
        drain(osend.at[clip, : n_seq - 1], o_ss.at[clip])
    drain(wbuf.at[: n_z - 1, 0, 0, 0, 0], w_ss.at[0])
    drain(wbuf.at[:, 0, 0, 0, : len(y_peers)], w_ss.at[1])
    drain(wbuf.at[:, :, 0, :, : n_x - 1], w_ss.at[2])
    drain(wbuf.at[:, :, 0], w_ss.at[3])


def dims_y_hi(dims):
    return Y_HI


def body(*args):
    (queries, key_rows, value_rows, query_tan, key_tan, value_tan, residual, residual_tan,
     cond_mask, time_index, gate_table, gate_slope, out_weight) = args
    clips, tok, width = queries.shape
    n_out = out_weight.shape[1]
    n_seq = lax.axis_size("seq")
    n_z = n_seq // GROUP
    n_x = lax.axis_size("fsdp") // Y_HI
    d = HEAD_DIM
    length = n_seq * tok
    rows = GROUP * tok
    steps = gate_table.shape[0]
    w_rows = out_weight.shape[0]
    anywhere = pl.BlockSpec(memory_space=pl.ANY)
    vmem = pl.BlockSpec(memory_space=pltpu.VMEM)
    smem = pl.BlockSpec(memory_space=pltpu.SMEM)
    out_shape = jax.ShapeDtypeStruct((clips, tok, n_out), NARROW)
    dma = pltpu.SemaphoreType.DMA
    return pl.pallas_call(
        functools.partial(kernel, (n_z, n_x, tok, n_out)),
        out_shape=(out_shape, out_shape),
        in_specs=[anywhere] * 8 + [vmem, smem] + [anywhere] * 3,
        out_specs=(vmem, vmem),
        scratch_shapes=[
            pltpu.VMEM((clips, 6, tok, width), NARROW),
            pltpu.VMEM((clips, n_seq, tok, 4 * d), NARROW),
            pltpu.VMEM((clips, length, 4 * d), NARROW),
            pltpu.VMEM((clips, n_seq, tok, 2 * d), NARROW),
            pltpu.VMEM((clips, length, 2 * d), NARROW),
            pltpu.VMEM((clips, n_seq, 2 * tok, d), NARROW),
            pltpu.VMEM((clips, n_seq, 2 * tok, d), NARROW),
            pltpu.VMEM((n_z, Y_LO, CORE, Y_HI, n_x, w_rows, n_out), NARROW),
            pltpu.VMEM((2, clips, tok, n_out), NARROW),
            pltpu.VMEM((2, steps, n_out), WIDE),
            pltpu.VMEM((2 * rows, length), WIDE),
            pltpu.VMEM((2 * rows, length), NARROW),
            pltpu.VMEM((rows, d), WIDE),
            pltpu.VMEM((2 * tok, width), NARROW),
            dma((clips, 6)), dma((4,)),
            dma((clips,)), dma((clips,)), dma((clips,)), dma((clips, n_z)), dma((clips,)), dma((clips,)),
            dma((4,)), dma((4,)), dma((1,)),
        ],
        compiler_params=pltpu.CompilerParams(
            collective_id=0, has_side_effects=True, vmem_limit_bytes=62 * 2**20
        ),
        cost_estimate=pl.CostEstimate(
            flops=20 * 10**9, bytes_accessed=12 * 2**20, transcendentals=8 * 2**20
        ),
    )(*args)


def solution(mesh):
    tokens = P("fsdp", "seq", None)
    in_specs = (tokens,) * 8 + (P("fsdp", "seq"), P("fsdp"), P(), P(), P(("seq", "fsdp"), None))
    return jax.shard_map(
        body, mesh=mesh, in_specs=in_specs, out_specs=(tokens, tokens), check_vma=False
    )
```

```python
import functools
import math

import jax
import jax.numpy as jnp
from jax import lax
from jax.experimental import pallas as pl
from jax.experimental.pallas import tpu as pltpu
from jax.sharding import PartitionSpec as P

HEAD_DIM = 128
Y_LO, CORE, Y_HI = 2, 2, 2
GROUP = Y_LO * CORE
EARLY_CHUNKS = 6
CLIPS = 2
NARROW = jnp.bfloat16
WIDE = jnp.float32


def column_of(row, length):
    square = (length, length)
    same = lax.broadcasted_iota(jnp.int32, square, 0) == lax.broadcasted_iota(jnp.int32, square, 1)
    return jnp.sum(jnp.where(same, jnp.broadcast_to(row, square), 0.0), 1, keepdims=True)


def kernel(
    dims,
    q_ref, k_ref, v_ref, qt_ref, kt_ref, vt_ref, res_ref, rest_ref,
    mask_ref, time_ref, gate_ref, slope_ref, weight_ref,
    out_ref, tan_ref,
    raw, kvsend, kvbuf, qsend, qbuf, osend, orecv, wbuf, resbuf, gatebuf,
    scores, probs, sums, joined,
    load_sem, res_sem, kv_ss, kv_rs, q_ss, q_rs, o_ss, o_rs, w_ss, w_rs, own_sem,
):
    n_z, n_x, tok, n_out = dims
    n_seq = n_z * GROUP
    length = n_seq * tok
    d = HEAD_DIM
    rows = GROUP * tok
    me = lax.axis_index("seq")
    my_f = lax.axis_index("fsdp")
    z, y_lo, core = me // GROUP, (me // CORE) % Y_LO, me % CORE
    y_hi, x = my_f // n_x, my_f % n_x
    y_hi_count = dims_y_hi(dims)

    def ring_z(step, sign):
        return (z + (2 * (step % 2) - 1) * ((step + 1) // 2) * sign + n_z) % n_z

    def seq_peer(slot, sign):
        pz = ring_z(slot // GROUP, sign)
        py = (y_lo + (slot // CORE) % Y_LO) % Y_LO
        pc = (core + slot) % CORE
        return pz * GROUP + py * CORE + pc

    def device(seq, fsdp):
        return {"seq": seq, "fsdp": fsdp}

    x_peers = [device(me, y_hi * n_x + (x + dx) % n_x) for dx in range(1, n_x)]
    y_peers = [
        device(
            z * GROUP + ((y_lo + a) % Y_LO) * CORE + core,
            ((y_hi + b) % y_hi_count) * n_x + x,
        )
        for b in range(y_hi_count)
        for a in range(Y_LO)
        if (a, b) != (0, 0)
    ]
    y_far = [p for p, (b, a) in zip(
        y_peers,
        [(b, a) for b in range(y_hi_count) for a in range(Y_LO) if (a, b) != (0, 0)],
    ) if b]

    streams = (k_ref, kt_ref, v_ref, vt_ref, qt_ref, q_ref)

    def load(clip, stream):
        return pltpu.make_async_copy(
            streams[stream].at[clip], raw.at[clip, stream], load_sem.at[clip, stream]
        )

    for clip in range(CLIPS):
        for stream in range(6):
            load(clip, stream).start()
    own_weight = pltpu.make_async_copy(weight_ref, wbuf.at[z, y_lo, core, y_hi, x], own_sem.at[0])
    own_weight.start()
    late_loads = [
        pltpu.make_async_copy(res_ref, resbuf.at[0], res_sem.at[0]),
        pltpu.make_async_copy(rest_ref, resbuf.at[1], res_sem.at[1]),
        pltpu.make_async_copy(gate_ref, gatebuf.at[0], res_sem.at[2]),
        pltpu.make_async_copy(slope_ref, gatebuf.at[1], res_sem.at[3]),
    ]

    barrier = pltpu.get_barrier_semaphore()

    def greet(slot, carry):
        pl.semaphore_signal(barrier, inc=1, device_id=device(seq_peer(slot, 1), my_f))
        return carry

    lax.fori_loop(1, n_seq, greet, 0)
    for peer in x_peers + y_far:
        pl.semaphore_signal(barrier, inc=1, device_id=peer)

    live = [
        column_of((mask_ref[pl.ds(clip, 1), :] == 0).astype(WIDE), tok) for clip in range(CLIPS)
    ]

    def send_kv(clip):
        for stream in range(4):
            load(clip, stream).wait()

        def one(slot, carry):
            peer = seq_peer(slot, 1)
            lanes = pl.ds(pl.multiple_of(peer * d, d), d)
            for stream in range(4):
                part = raw[clip, stream, :, lanes]
                if stream % 2:
                    part = (part.astype(WIDE) * live[clip]).astype(NARROW)
                kvsend[clip, peer, :, stream * d : (stream + 1) * d] = part

            @pl.when(slot != 0)
            def _():
                pltpu.make_async_remote_copy(
                    src_ref=kvsend.at[clip, peer],
                    dst_ref=kvbuf.at[clip, pl.ds(pl.multiple_of(slot * tok, tok), tok)],
                    send_sem=kv_ss.at[clip],
                    recv_sem=kv_rs.at[clip],
                    device_id=device(peer, my_f),
                ).start()

            return carry

        lax.fori_loop(0, n_seq, one, 0)
        kvbuf[clip, :tok] = kvsend[clip, me]

    def send_q(clip):
        for stream in range(4, 6):
            load(clip, stream).wait()

        def one(slot, carry):
            peer = seq_peer(slot, 1)
            lanes = pl.ds(pl.multiple_of(peer * d, d), d)
            part = raw[clip, 4, :, lanes]
            qsend[clip, peer, :, :d] = (part.astype(WIDE) * live[clip]).astype(NARROW)
            qsend[clip, peer, :, d:] = raw[clip, 5, :, lanes]

            @pl.when(slot != 0)
            def _():
                pltpu.make_async_remote_copy(
                    src_ref=qsend.at[clip, peer],
                    dst_ref=qbuf.at[clip, pl.ds(pl.multiple_of(slot * tok, tok), tok)],
                    send_sem=q_ss.at[clip],
                    recv_sem=q_rs.at[clip, slot // GROUP],
                    device_id=device(peer, my_f),
                ).start()

            return carry

        lax.fori_loop(0, n_seq, one, 0)
        qbuf[clip, :tok] = qsend[clip, me]

    def drain(ref, sem):
        pltpu.make_async_copy(ref, ref, sem).wait()

    pl.semaphore_wait(barrier, n_seq - 1 + len(x_peers) + len(y_far))

    def spread_z(step, carry):
        pltpu.make_async_remote_copy(
            src_ref=weight_ref, dst_ref=wbuf.at[z, y_lo, core, y_hi, x],
            send_sem=w_ss.at[0], recv_sem=w_rs.at[0, step],
            device_id=device(ring_z(step, 1) * GROUP + y_lo * CORE + core, my_f),
        ).start()
        return carry

    def spread_y(step):
        part = wbuf.at[ring_z(step, -1), y_lo, core, y_hi, x]
        for peer in y_peers:
            pltpu.make_async_remote_copy(
                src_ref=part, dst_ref=part, send_sem=w_ss.at[1], recv_sem=w_rs.at[1, step],
                device_id=peer,
            ).start()

    def spread_x(step):
        drain(wbuf.at[0, 0, 0, 0, : len(y_peers)], w_rs.at[1, step])
        part = wbuf.at[ring_z(step, -1), :, core, :, x]
        for peer in x_peers:
            pltpu.make_async_remote_copy(
                src_ref=part, dst_ref=part, send_sem=w_ss.at[2], recv_sem=w_rs.at[2, step],
                device_id=peer,
            ).start()

    def spread_core(step, carry):
        drain(wbuf.at[0, :, 0, :, : n_x - 1], w_rs.at[2, step])
        part = wbuf.at[ring_z(step, -1), :, core]
        pltpu.make_async_remote_copy(
            src_ref=part, dst_ref=part, send_sem=w_ss.at[3], recv_sem=w_rs.at[3, step],
            device_id=device(z * GROUP + y_lo * CORE + (core + 1) % CORE, my_f),
        ).start()
        return carry

    lax.fori_loop(1, n_z, spread_z, 0)
    own_weight.wait()
    spread_y(0)
    send_kv(0)
    send_q(0)
    send_kv(1)
    send_q(1)
    for copy in late_loads:
        copy.start()

    def spread_yx(step, carry):
        drain(wbuf.at[0, 0, 0, 0, 0], w_rs.at[0, step])
        spread_y(step)
        spread_x(step - 1)
        return carry

    lax.fori_loop(1, n_z, spread_yx, 0)
    spread_x(n_z - 1)

    scale = d ** (-0.5)
    to_exponent = scale * math.log2(math.e)
    step_rows = 16

    def attend(clip):
        drain(kvbuf.at[clip, tok:], kv_rs.at[clip])

        def block(index, carry):
            start = pl.multiple_of(index * rows, rows)

            @pl.when(index == 0)
            def _():
                drain(qbuf.at[clip, tok:rows], q_rs.at[clip, 0])

            @pl.when(index != 0)
            def _():
                drain(qbuf.at[clip, pl.ds(start, rows)], q_rs.at[clip, index])

            both = qbuf[clip, pl.ds(start, rows)]
            plain = both[:, d:]
            left = jnp.concatenate(
                [jnp.concatenate([plain, jnp.zeros_like(plain)], 1), both], 0
            )
            scores[...] = lax.dot_general(
                left, kvbuf[clip, :, : 2 * d], (((1,), (1,)), ((), ())),
                preferred_element_type=WIDE,
            )

            def soften(step, carry):
                at = pl.multiple_of(step * step_rows, step_rows)
                exponent = scores[pl.ds(at, step_rows)] * to_exponent
                weight = jnp.exp2(exponent - jnp.max(exponent, 1, keepdims=True))
                total = jnp.sum(weight, 1, keepdims=True)
                slant = scores[pl.ds(rows + at, step_rows)]
                centre = jnp.sum(weight * slant, 1, keepdims=True) / total
                probs[pl.ds(at, step_rows)] = weight.astype(NARROW)
                probs[pl.ds(rows + at, step_rows)] = (weight * (slant - centre)).astype(NARROW)
                sums[pl.ds(at, step_rows)] = jnp.broadcast_to(1.0 / total, (step_rows, d))
                return carry

            lax.fori_loop(0, rows // step_rows, soften, 0)
            result = jnp.dot(
                probs[...], kvbuf[clip, :, 2 * d :], preferred_element_type=WIDE
            )
            inverse = sums[...]
            value = (result[:rows, :d] * inverse).astype(NARROW)
            value_tan = (
                (result[rows:, :d] * scale + result[:rows, d:]) * inverse
            ).astype(NARROW)
            for part in range(GROUP):
                slot = index * GROUP + part
                at = slice(part * tok, (part + 1) * tok)
                osend[clip, slot, :tok] = value[at]
                osend[clip, slot, tok:] = value_tan[at]
            for part in range(GROUP):
                slot = index * GROUP + part
                copy = pltpu.make_async_remote_copy(
                    src_ref=osend.at[clip, slot],
                    dst_ref=orecv.at[clip, me],
                    send_sem=o_ss.at[clip],
                    recv_sem=o_rs.at[clip],
                    device_id=device(seq_peer(slot, -1), my_f),
                )
                if part:
                    copy.start()
                else:
                    pl.when(index != 0)(copy.start)
            return carry

        lax.fori_loop(0, n_z, block, 0)
        orecv[clip, me] = osend[clip, 0]

    attend(0)
    lax.fori_loop(0, EARLY_CHUNKS, spread_core, 0)
    attend(1)
    lax.fori_loop(EARLY_CHUNKS, n_z, spread_core, 0)

    def settle(step, carry):
        drain(wbuf.at[0, :, 0], w_rs.at[3, step])
        return carry

    lax.fori_loop(0, n_z, settle, 0)
    for copy in late_loads:
        copy.wait()

    tile = 256
    steps = gatebuf.shape[1]

    def project(clip):
        drain(orecv.at[clip, : n_seq - 1], o_rs.at[clip])
        for head in range(n_seq):
            joined[:, head * d : (head + 1) * d] = orecv[clip, head]
        picked = (
            lax.broadcasted_iota(jnp.int32, (steps, 1), 0) == time_ref[clip]
        ).astype(WIDE)

        def one(index, carry):
            lanes = pl.ds(pl.multiple_of(index * tile, tile), tile)
            weight = wbuf[:, :, :, :, :, :, lanes].reshape(n_seq * d, tile)
            both = jnp.dot(joined[...], weight, preferred_element_type=WIDE)
            gate = jnp.sum(gatebuf[0, :, lanes] * picked, 0, keepdims=True)
            slope = jnp.sum(gatebuf[1, :, lanes] * picked, 0, keepdims=True)
            plain, tangent = both[:tok], both[tok:]
            out_ref[clip, :, lanes] = (
                resbuf[0, clip, :, lanes].astype(WIDE) + gate * plain
            ).astype(NARROW)
            tan_ref[clip, :, lanes] = (
                resbuf[1, clip, :, lanes].astype(WIDE) * live[clip] + slope * plain + gate * tangent
            ).astype(NARROW)
            return carry

        lax.fori_loop(0, n_out // tile, one, 0)

    project(0)
    project(1)

    for clip in range(CLIPS):
        drain(kvsend.at[clip, : n_seq - 1], kv_ss.at[clip])
        drain(qsend.at[clip, : n_seq - 1], q_ss.at[clip])
        drain(osend.at[clip, : n_seq - 1], o_ss.at[clip])
    drain(wbuf.at[: n_z - 1, 0, 0, 0, 0], w_ss.at[0])
    drain(wbuf.at[:, 0, 0, 0, : len(y_peers)], w_ss.at[1])
    drain(wbuf.at[:, :, 0, :, : n_x - 1], w_ss.at[2])
    drain(wbuf.at[:, :, 0], w_ss.at[3])


def dims_y_hi(dims):
    return Y_HI


def body(*args):
    (queries, key_rows, value_rows, query_tan, key_tan, value_tan, residual, residual_tan,
     cond_mask, time_index, gate_table, gate_slope, out_weight) = args
    clips, tok, width = queries.shape
    n_out = out_weight.shape[1]
    n_seq = lax.axis_size("seq")
    n_z = n_seq // GROUP
    n_x = lax.axis_size("fsdp") // Y_HI
    d = HEAD_DIM
    length = n_seq * tok
    rows = GROUP * tok
    steps = gate_table.shape[0]
    w_rows = out_weight.shape[0]
    anywhere = pl.BlockSpec(memory_space=pl.ANY)
    vmem = pl.BlockSpec(memory_space=pltpu.VMEM)
    smem = pl.BlockSpec(memory_space=pltpu.SMEM)
    out_shape = jax.ShapeDtypeStruct((clips, tok, n_out), NARROW)
    dma = pltpu.SemaphoreType.DMA
    return pl.pallas_call(
        functools.partial(kernel, (n_z, n_x, tok, n_out)),
        out_shape=(out_shape, out_shape),
        in_specs=[anywhere] * 8 + [vmem, smem] + [anywhere] * 3,
        out_specs=(vmem, vmem),
        scratch_shapes=[
            pltpu.VMEM((clips, 6, tok, width), NARROW),
            pltpu.VMEM((clips, n_seq, tok, 4 * d), NARROW),
            pltpu.VMEM((clips, length, 4 * d), NARROW),
            pltpu.VMEM((clips, n_seq, tok, 2 * d), NARROW),
            pltpu.VMEM((clips, length, 2 * d), NARROW),
            pltpu.VMEM((clips, n_seq, 2 * tok, d), NARROW),
            pltpu.VMEM((clips, n_seq, 2 * tok, d), NARROW),
            pltpu.VMEM((n_z, Y_LO, CORE, Y_HI, n_x, w_rows, n_out), NARROW),
            pltpu.VMEM((2, clips, tok, n_out), NARROW),
            pltpu.VMEM((2, steps, n_out), WIDE),
            pltpu.VMEM((2 * rows, length), WIDE),
            pltpu.VMEM((2 * rows, length), NARROW),
            pltpu.VMEM((rows, d), WIDE),
            pltpu.VMEM((2 * tok, width), NARROW),
            dma((clips, 6)), dma((4,)),
            dma((clips,)), dma((clips,)), dma((clips,)), dma((clips, n_z)), dma((clips,)), dma((clips,)),
            dma((4,)), dma((4, n_z)), dma((1,)),
        ],
        compiler_params=pltpu.CompilerParams(
            collective_id=0, has_side_effects=True, vmem_limit_bytes=62 * 2**20
        ),
        cost_estimate=pl.CostEstimate(
            flops=20 * 10**9, bytes_accessed=12 * 2**20, transcendentals=8 * 2**20
        ),
    )(*args)


def solution(mesh):
    tokens = P("fsdp", "seq", None)
    in_specs = (tokens,) * 8 + (P("fsdp", "seq"), P("fsdp"), P(), P(), P(("seq", "fsdp"), None))
    return jax.shard_map(
        body, mesh=mesh, in_specs=in_specs, out_specs=(tokens, tokens), check_vma=False
    )
```

```python
import functools
import math

import jax
import jax.numpy as jnp
from jax import lax
from jax.experimental import pallas as pl
from jax.experimental.pallas import tpu as pltpu
from jax.sharding import PartitionSpec as P

HEAD_DIM = 128
Y_LO, CORE, Y_HI = 2, 2, 2
GROUP = Y_LO * CORE
EARLY_CHUNKS = 6
CLIPS = 2
NARROW = jnp.bfloat16
WIDE = jnp.float32


def column_of(row, length):
    square = (length, length)
    same = lax.broadcasted_iota(jnp.int32, square, 0) == lax.broadcasted_iota(jnp.int32, square, 1)
    return jnp.sum(jnp.where(same, jnp.broadcast_to(row, square), 0.0), 1, keepdims=True)


def kernel(
    dims,
    q_ref, k_ref, v_ref, qt_ref, kt_ref, vt_ref, res_ref, rest_ref,
    mask_ref, time_ref, gate_ref, slope_ref, weight_ref,
    out_ref, tan_ref,
    raw, kvsend, kvbuf, qsend, qbuf, osend, orecv, wbuf, resbuf, gatebuf,
    scores, probs, sums, joined, total,
    load_sem, res_sem, kv_ss, kv_rs, q_ss, q_rs, o_ss, o_rs, w_ss, w_rs, own_sem,
):
    n_z, n_x, tok, n_out = dims
    n_seq = n_z * GROUP
    length = n_seq * tok
    d = HEAD_DIM
    rows = GROUP * tok
    me = lax.axis_index("seq")
    my_f = lax.axis_index("fsdp")
    z, y_lo, core = me // GROUP, (me // CORE) % Y_LO, me % CORE
    y_hi, x = my_f // n_x, my_f % n_x
    y_hi_count = dims_y_hi(dims)

    def ring_z(step, sign):
        return (z + (2 * (step % 2) - 1) * ((step + 1) // 2) * sign + n_z) % n_z

    def seq_peer(slot, sign):
        pz = ring_z(n_z - 1 - slot // GROUP, sign)
        py = (y_lo + (slot // CORE) % Y_LO) % Y_LO
        pc = (core + slot) % CORE
        return pz * GROUP + py * CORE + pc

    own_slot = (n_z - 1) * GROUP
    own_rows = slice(own_slot * tok, (own_slot + 1) * tok)

    def device(seq, fsdp):
        return {"seq": seq, "fsdp": fsdp}

    x_peers = [device(me, y_hi * n_x + (x + dx) % n_x) for dx in range(1, n_x)]
    y_peers = [
        device(
            z * GROUP + ((y_lo + a) % Y_LO) * CORE + core,
            ((y_hi + b) % y_hi_count) * n_x + x,
        )
        for b in range(y_hi_count)
        for a in range(Y_LO)
        if (a, b) != (0, 0)
    ]
    y_far = [p for p, (b, a) in zip(
        y_peers,
        [(b, a) for b in range(y_hi_count) for a in range(Y_LO) if (a, b) != (0, 0)],
    ) if b]

    streams = (k_ref, kt_ref, v_ref, vt_ref, qt_ref, q_ref)

    def load(clip, stream):
        return pltpu.make_async_copy(
            streams[stream].at[clip], raw.at[clip, stream], load_sem.at[clip, stream]
        )

    for clip in range(CLIPS):
        for stream in range(6):
            load(clip, stream).start()
    own_weight = pltpu.make_async_copy(weight_ref, wbuf.at[z, y_lo, core, y_hi, x], own_sem.at[0])
    own_weight.start()
    late_loads = [
        pltpu.make_async_copy(res_ref, resbuf.at[0], res_sem.at[0]),
        pltpu.make_async_copy(rest_ref, resbuf.at[1], res_sem.at[1]),
        pltpu.make_async_copy(gate_ref, gatebuf.at[0], res_sem.at[2]),
        pltpu.make_async_copy(slope_ref, gatebuf.at[1], res_sem.at[3]),
    ]

    barrier = pltpu.get_barrier_semaphore()

    def greet(step, carry):
        pl.semaphore_signal(barrier, inc=1, device_id=device((me + step) % n_seq, my_f))
        return carry

    lax.fori_loop(1, n_seq, greet, 0)
    for peer in x_peers + y_far:
        pl.semaphore_signal(barrier, inc=1, device_id=peer)

    live = [
        column_of((mask_ref[pl.ds(clip, 1), :] == 0).astype(WIDE), tok) for clip in range(CLIPS)
    ]

    def await_kv(clip):
        for stream in range(4):
            load(clip, stream).wait()

    def send_kv(clip, first, last):
        def one(slot, carry):
            peer = seq_peer(slot, 1)
            lanes = pl.ds(pl.multiple_of(peer * d, d), d)
            for stream in range(4):
                part = raw[clip, stream, :, lanes]
                if stream % 2:
                    part = (part.astype(WIDE) * live[clip]).astype(NARROW)
                kvsend[clip, peer, :, stream * d : (stream + 1) * d] = part

            @pl.when(slot != own_slot)
            def _():
                pltpu.make_async_remote_copy(
                    src_ref=kvsend.at[clip, peer],
                    dst_ref=kvbuf.at[clip, pl.ds(pl.multiple_of(slot * tok, tok), tok)],
                    send_sem=kv_ss.at[clip],
                    recv_sem=kv_rs.at[clip],
                    device_id=device(peer, my_f),
                ).start()

            return carry

        lax.fori_loop(first, last, one, 0)
        if last == n_seq:
            kvbuf[clip, own_rows] = kvsend[clip, me]

    def send_q(clip):
        for stream in range(4, 6):
            load(clip, stream).wait()

        def one(slot, carry):
            peer = seq_peer(slot, 1)
            lanes = pl.ds(pl.multiple_of(peer * d, d), d)
            part = raw[clip, 4, :, lanes]
            qsend[clip, peer, :, :d] = (part.astype(WIDE) * live[clip]).astype(NARROW)
            qsend[clip, peer, :, d:] = raw[clip, 5, :, lanes]

            @pl.when(slot != own_slot)
            def _():
                pltpu.make_async_remote_copy(
                    src_ref=qsend.at[clip, peer],
                    dst_ref=qbuf.at[clip, pl.ds(pl.multiple_of(slot * tok, tok), tok)],
                    send_sem=q_ss.at[clip],
                    recv_sem=q_rs.at[clip, slot // GROUP],
                    device_id=device(peer, my_f),
                ).start()

            return carry

        lax.fori_loop(0, n_seq, one, 0)
        qbuf[clip, own_rows] = qsend[clip, me]

    def drain(ref, sem):
        pltpu.make_async_copy(ref, ref, sem).wait()

    pl.semaphore_wait(barrier, n_seq - 1 + len(x_peers) + len(y_far))

    def to_neighbour(sign, part, step):
        pltpu.make_async_remote_copy(
            src_ref=part, dst_ref=part, send_sem=w_ss.at[0], recv_sem=w_rs.at[0, step],
            device_id=device(ring_z(1, sign) * GROUP + y_lo * CORE + core, my_f),
        ).start()

    def relay(far):
        for side, sign in ((2 * far - 1, 1), (2 * far, -1)):
            part = wbuf.at[ring_z(side, -1), y_lo, core, y_hi, x]
            drain(part, w_rs.at[0, side])
            if 2 * far + 2 < n_z:
                to_neighbour(sign, part, side + 2)
            else:
                half = part.shape[1] // 2
                lanes = slice(0, half) if sign == 1 else slice(half, 2 * half)
                to_neighbour(sign, part.at[:, lanes], 2 * far + 1)

    def spread_y(step):
        part = wbuf.at[ring_z(step, -1), y_lo, core, y_hi, x]
        for peer in y_peers:
            pltpu.make_async_remote_copy(
                src_ref=part, dst_ref=part, send_sem=w_ss.at[1], recv_sem=w_rs.at[1, step],
                device_id=peer,
            ).start()

    def spread_x(step):
        drain(wbuf.at[0, 0, 0, 0, : len(y_peers)], w_rs.at[1, step])
        part = wbuf.at[ring_z(step, -1), :, core, :, x]
        for peer in x_peers:
            pltpu.make_async_remote_copy(
                src_ref=part, dst_ref=part, send_sem=w_ss.at[2], recv_sem=w_rs.at[2, step],
                device_id=peer,
            ).start()

    def spread_core(step, carry):
        drain(wbuf.at[0, :, 0, :, : n_x - 1], w_rs.at[2, step])
        part = wbuf.at[ring_z(step, -1), :, core]
        pltpu.make_async_remote_copy(
            src_ref=part, dst_ref=part, send_sem=w_ss.at[3], recv_sem=w_rs.at[3, step],
            device_id=device(z * GROUP + y_lo * CORE + (core + 1) % CORE, my_f),
        ).start()
        return carry

    own_weight.wait()
    mine = wbuf.at[z, y_lo, core, y_hi, x]
    to_neighbour(1, mine, 1)
    to_neighbour(-1, mine, 2)
    spread_y(0)
    await_kv(0)
    hops = n_z // 2
    send_kv(0, 0, GROUP)
    for far in range(1, hops):
        relay(far)
        spread_y(2 * far - 1)
        spread_y(2 * far)
        for step in range(max(2 * far - 5, 0), 2 * far - 3):
            spread_x(step)
        send_kv(0, (2 * far - 1) * GROUP, (2 * far + 1) * GROUP)
    send_kv(0, (n_z - 1) * GROUP, n_seq)
    drain(wbuf.at[0, 0, 0, 0, 0], w_rs.at[0, n_z - 1])
    spread_y(n_z - 1)
    send_q(0)

    def continue_x(step, carry):
        spread_x(step)
        return carry

    lax.fori_loop(n_z - 5, n_z, continue_x, 0)
    await_kv(1)
    send_kv(1, 0, n_seq)
    send_q(1)
    for copy in late_loads:
        copy.start()

    scale = d ** (-0.5)
    to_exponent = scale * math.log2(math.e)
    step_rows = 16

    def give_back(clip, index):
        for part in range(GROUP):
            slot = index * GROUP + part
            copy = pltpu.make_async_remote_copy(
                src_ref=osend.at[clip, slot],
                dst_ref=orecv.at[clip, me],
                send_sem=o_ss.at[clip],
                recv_sem=o_rs.at[clip, index],
                device_id=device(seq_peer(slot, -1), my_f),
            )
            if part:
                copy.start()
            else:
                pl.when(index != n_z - 1)(copy.start)

    def attend(clip):
        drain(kvbuf.at[clip, tok:], kv_rs.at[clip])

        def block(index, carry):
            start = pl.multiple_of(index * rows, rows)

            @pl.when(index == n_z - 1)
            def _():
                drain(qbuf.at[clip, tok:rows], q_rs.at[clip, index])

            @pl.when(index != n_z - 1)
            def _():
                drain(qbuf.at[clip, :rows], q_rs.at[clip, index])

            if clip:
                give_back(clip - 1, index)
            both = qbuf[clip, pl.ds(start, rows)]
            plain = both[:, d:]
            left = jnp.concatenate(
                [jnp.concatenate([plain, jnp.zeros_like(plain)], 1), both], 0
            )
            scores[...] = lax.dot_general(
                left, kvbuf[clip, :, : 2 * d], (((1,), (1,)), ((), ())),
                preferred_element_type=WIDE,
            )

            def soften(step, carry):
                at = pl.multiple_of(step * step_rows, step_rows)
                exponent = scores[pl.ds(at, step_rows)] * to_exponent
                weight = jnp.exp2(exponent - jnp.max(exponent, 1, keepdims=True))
                norm = jnp.sum(weight, 1, keepdims=True)
                slant = scores[pl.ds(rows + at, step_rows)]
                centre = jnp.sum(weight * slant, 1, keepdims=True) / norm
                probs[pl.ds(at, step_rows)] = weight.astype(NARROW)
                probs[pl.ds(rows + at, step_rows)] = (weight * (slant - centre)).astype(NARROW)
                sums[pl.ds(at, step_rows)] = jnp.broadcast_to(1.0 / norm, (step_rows, d))
                return carry

            lax.fori_loop(0, rows // step_rows, soften, 0, unroll=4)
            result = jnp.dot(
                probs[...], kvbuf[clip, :, 2 * d :], preferred_element_type=WIDE
            )
            inverse = sums[...]
            value = (result[:rows, :d] * inverse).astype(NARROW)
            value_tan = (
                (result[rows:, :d] * scale + result[:rows, d:]) * inverse
            ).astype(NARROW)
            for part in range(GROUP):
                slot = index * GROUP + part
                at = slice(part * tok, (part + 1) * tok)
                osend[clip, slot, :tok] = value[at]
                osend[clip, slot, tok:] = value_tan[at]
            if clip == CLIPS - 1:
                give_back(clip, index)
            return carry

        lax.fori_loop(0, n_z, block, 0)
        orecv[clip, me] = osend[clip, own_slot]

    attend(0)
    lax.fori_loop(0, EARLY_CHUNKS, spread_core, 0)
    attend(1)
    lax.fori_loop(EARLY_CHUNKS, n_z, spread_core, 0)

    def settle(step, carry):
        drain(wbuf.at[0, :, 0], w_rs.at[3, step])
        return carry

    lax.fori_loop(0, n_z, settle, 0)
    for copy in late_loads:
        copy.wait()

    tile = 512
    depth = GROUP * d
    steps = gatebuf.shape[1]

    picked = [
        (lax.broadcasted_iota(jnp.int32, (steps, 1), 0) == time_ref[clip]).astype(WIDE)
        for clip in range(CLIPS)
    ]

    def gather(step):
        at = ring_z(n_z - 1 - step, 1)
        for clip in range(CLIPS):
            for part in range(GROUP):
                joined[clip * 2 * tok : (clip + 1) * 2 * tok, part * d : (part + 1) * d] = orecv[
                    clip, at * GROUP + part
                ]
        return at

    def product(at, index):
        lanes = pl.ds(pl.multiple_of(index * tile, tile), tile)
        weight = wbuf[at, :, :, :, :, :, lanes].reshape(depth, tile)
        return lanes, jnp.dot(joined[...], weight, preferred_element_type=WIDE)

    def project(step, carry):
        for clip in range(CLIPS):
            drain(orecv.at[clip, :GROUP], o_rs.at[clip, step])
        at = gather(step)

        def one(index, carry):
            lanes, both = product(at, index)

            @pl.when(step == 0)
            def _():
                total[:, lanes] = both

            @pl.when(step != 0)
            def _():
                total[:, lanes] += both

            return carry

        lax.fori_loop(0, n_out // tile, one, 0, unroll=True)
        return carry

    lax.fori_loop(0, n_z - 1, project, 0)
    for clip in range(CLIPS):
        drain(orecv.at[clip, : GROUP - 1], o_rs.at[clip, n_z - 1])
    nearest = gather(n_z - 1)

    def finish(index, carry):
        lanes, both = product(nearest, index)
        both = total[:, lanes] + both
        for clip in range(CLIPS):
            gate = jnp.sum(gatebuf[0, :, lanes] * picked[clip], 0, keepdims=True)
            slope = jnp.sum(gatebuf[1, :, lanes] * picked[clip], 0, keepdims=True)
            at = clip * 2 * tok
            plain, tangent = both[at : at + tok], both[at + tok : at + 2 * tok]
            out_ref[clip, :, lanes] = (
                resbuf[0, clip, :, lanes].astype(WIDE) + gate * plain
            ).astype(NARROW)
            tan_ref[clip, :, lanes] = (
                resbuf[1, clip, :, lanes].astype(WIDE) * live[clip] + slope * plain + gate * tangent
            ).astype(NARROW)
        return carry

    lax.fori_loop(0, n_out // tile, finish, 0, unroll=True)

    for clip in range(CLIPS):
        drain(kvsend.at[clip, : n_seq - 1], kv_ss.at[clip])
        drain(qsend.at[clip, : n_seq - 1], q_ss.at[clip])
        drain(osend.at[clip, : n_seq - 1], o_ss.at[clip])
    drain(wbuf.at[: n_z - 1, 0, 0, 0, 0], w_ss.at[0])
    drain(wbuf.at[:, 0, 0, 0, : len(y_peers)], w_ss.at[1])
    drain(wbuf.at[:, :, 0, :, : n_x - 1], w_ss.at[2])
    drain(wbuf.at[:, :, 0], w_ss.at[3])


def dims_y_hi(dims):
    return Y_HI


def body(*args):
    (queries, key_rows, value_rows, query_tan, key_tan, value_tan, residual, residual_tan,
     cond_mask, time_index, gate_table, gate_slope, out_weight) = args
    clips, tok, width = queries.shape
    n_out = out_weight.shape[1]
    n_seq = lax.axis_size("seq")
    n_z = n_seq // GROUP
    n_x = lax.axis_size("fsdp") // Y_HI
    d = HEAD_DIM
    length = n_seq * tok
    rows = GROUP * tok
    steps = gate_table.shape[0]
    w_rows = out_weight.shape[0]
    anywhere = pl.BlockSpec(memory_space=pl.ANY)
    vmem = pl.BlockSpec(memory_space=pltpu.VMEM)
    smem = pl.BlockSpec(memory_space=pltpu.SMEM)
    out_shape = jax.ShapeDtypeStruct((clips, tok, n_out), NARROW)
    dma = pltpu.SemaphoreType.DMA
    return pl.pallas_call(
        functools.partial(kernel, (n_z, n_x, tok, n_out)),
        out_shape=(out_shape, out_shape),
        in_specs=[anywhere] * 8 + [vmem, smem] + [anywhere] * 3,
        out_specs=(vmem, vmem),
        scratch_shapes=[
            pltpu.VMEM((clips, 6, tok, width), NARROW),
            pltpu.VMEM((clips, n_seq, tok, 4 * d), NARROW),
            pltpu.VMEM((clips, length, 4 * d), NARROW),
            pltpu.VMEM((clips, n_seq, tok, 2 * d), NARROW),
            pltpu.VMEM((clips, length, 2 * d), NARROW),
            pltpu.VMEM((clips, n_seq, 2 * tok, d), NARROW),
            pltpu.VMEM((clips, n_seq, 2 * tok, d), NARROW),
            pltpu.VMEM((n_z, Y_LO, CORE, Y_HI, n_x, w_rows, n_out), NARROW),
            pltpu.VMEM((2, clips, tok, n_out), NARROW),
            pltpu.VMEM((2, steps, n_out), WIDE),
            pltpu.VMEM((2 * rows, length), WIDE),
            pltpu.VMEM((2 * rows, length), NARROW),
            pltpu.VMEM((rows, d), WIDE),
            pltpu.VMEM((clips * 2 * tok, GROUP * d), NARROW),
            pltpu.VMEM((clips * 2 * tok, n_out), WIDE),
            dma((clips, 6)), dma((4,)),
            dma((clips,)), dma((clips,)), dma((clips,)), dma((clips, n_z)), dma((clips,)), dma((clips, n_z)),
            dma((4,)), dma((4, n_z)), dma((1,)),
        ],
        compiler_params=pltpu.CompilerParams(
            collective_id=0, has_side_effects=True, vmem_limit_bytes=62 * 2**20
        ),
        cost_estimate=pl.CostEstimate(
            flops=20 * 10**9, bytes_accessed=12 * 2**20, transcendentals=8 * 2**20
        ),
    )(*args)


def solution(mesh):
    tokens = P("fsdp", "seq", None)
    in_specs = (tokens,) * 8 + (P("fsdp", "seq"), P("fsdp"), P(), P(), P(("seq", "fsdp"), None))
    return jax.shard_map(
        body, mesh=mesh, in_specs=in_specs, out_specs=(tokens, tokens), check_vma=False
    )
```

```python
import functools
import math

import jax
import jax.numpy as jnp
from jax import lax
from jax.experimental import pallas as pl
from jax.experimental.pallas import tpu as pltpu
from jax.sharding import PartitionSpec as P

HEAD_DIM = 128
Y_LO, CORE, Y_HI = 2, 2, 2
GROUP = Y_LO * CORE
EARLY_CHUNKS = 6
CLIPS = 2
NARROW = jnp.bfloat16
WIDE = jnp.float32


def column_of(row, length):
    square = (length, length)
    same = lax.broadcasted_iota(jnp.int32, square, 0) == lax.broadcasted_iota(jnp.int32, square, 1)
    return jnp.sum(jnp.where(same, jnp.broadcast_to(row, square), 0.0), 1, keepdims=True)


def kernel(
    dims,
    q_ref, k_ref, v_ref, qt_ref, kt_ref, vt_ref, res_ref, rest_ref,
    mask_ref, time_ref, gate_ref, slope_ref, weight_ref,
    out_ref, tan_ref,
    raw, kvsend, kvbuf, qsend, qbuf, osend, orecv, wbuf, resbuf, gatebuf,
    scores, probs, sums, joined, total, outbuf,
    load_sem, res_sem, kv_ss, kv_rs, q_ss, q_rs, o_ss, o_rs, w_ss, w_rs, own_sem, store_sem,
):
    n_z, n_x, tok, n_out = dims
    n_seq = n_z * GROUP
    length = n_seq * tok
    d = HEAD_DIM
    rows = GROUP * tok
    me = lax.axis_index("seq")
    my_f = lax.axis_index("fsdp")
    z, y_lo, core = me // GROUP, (me // CORE) % Y_LO, me % CORE
    y_hi, x = my_f // n_x, my_f % n_x
    y_hi_count = dims_y_hi(dims)

    def ring_z(step, sign):
        return (z + (2 * (step % 2) - 1) * ((step + 1) // 2) * sign + n_z) % n_z

    def seq_peer(slot, sign):
        pz = ring_z(n_z - 1 - slot // GROUP, sign)
        py = (y_lo + (slot // CORE) % Y_LO) % Y_LO
        pc = (core + slot) % CORE
        return pz * GROUP + py * CORE + pc

    own_slot = (n_z - 1) * GROUP
    own_rows = slice(own_slot * tok, (own_slot + 1) * tok)

    def device(seq, fsdp):
        return {"seq": seq, "fsdp": fsdp}

    x_peers = [device(me, y_hi * n_x + (x + dx) % n_x) for dx in range(1, n_x)]
    y_peers = [
        device(
            z * GROUP + ((y_lo + a) % Y_LO) * CORE + core,
            ((y_hi + b) % y_hi_count) * n_x + x,
        )
        for b in range(y_hi_count)
        for a in range(Y_LO)
        if (a, b) != (0, 0)
    ]
    y_far = [p for p, (b, a) in zip(
        y_peers,
        [(b, a) for b in range(y_hi_count) for a in range(Y_LO) if (a, b) != (0, 0)],
    ) if b]

    barrier = pltpu.get_barrier_semaphore()

    def greet(step, carry):
        pl.semaphore_signal(barrier, inc=1, device_id=device((me + step) % n_seq, my_f))
        return carry

    lax.fori_loop(1, n_seq, greet, 0)
    for peer in x_peers + y_far:
        pl.semaphore_signal(barrier, inc=1, device_id=peer)

    streams = (k_ref, kt_ref, v_ref, vt_ref, qt_ref, q_ref)

    def load(clip, stream):
        return pltpu.make_async_copy(
            streams[stream].at[clip], raw.at[clip, stream], load_sem.at[clip, stream]
        )

    for clip in range(CLIPS):
        for stream in range(6):
            load(clip, stream).start()
    own_weight = pltpu.make_async_copy(weight_ref, wbuf.at[z, y_lo, core, y_hi, x], own_sem.at[0])
    own_weight.start()
    late_loads = [
        pltpu.make_async_copy(res_ref, resbuf.at[0], res_sem.at[0]),
        pltpu.make_async_copy(rest_ref, resbuf.at[1], res_sem.at[1]),
        pltpu.make_async_copy(gate_ref, gatebuf.at[0], res_sem.at[2]),
        pltpu.make_async_copy(slope_ref, gatebuf.at[1], res_sem.at[3]),
    ]

    live = [
        column_of((mask_ref[pl.ds(clip, 1), :] == 0).astype(WIDE), tok) for clip in range(CLIPS)
    ]

    def await_kv(clip):
        for stream in range(4):
            load(clip, stream).wait()

    def send_kv(clip, first, last):
        def one(slot, carry):
            peer = seq_peer(slot, 1)
            lanes = pl.ds(pl.multiple_of(peer * d, d), d)
            for stream in range(4):
                part = raw[clip, stream, :, lanes]
                if stream % 2:
                    part = (part.astype(WIDE) * live[clip]).astype(NARROW)
                kvsend[clip, peer, :, stream * d : (stream + 1) * d] = part

            @pl.when(slot != own_slot)
            def _():
                pltpu.make_async_remote_copy(
                    src_ref=kvsend.at[clip, peer],
                    dst_ref=kvbuf.at[clip, pl.ds(pl.multiple_of(slot * tok, tok), tok)],
                    send_sem=kv_ss.at[clip],
                    recv_sem=kv_rs.at[clip],
                    device_id=device(peer, my_f),
                ).start()

            return carry

        lax.fori_loop(first, last, one, 0)
        if last == n_seq:
            kvbuf[clip, own_rows] = kvsend[clip, me]

    def send_q(clip):
        for stream in range(4, 6):
            load(clip, stream).wait()

        def one(slot, carry):
            peer = seq_peer(slot, 1)
            lanes = pl.ds(pl.multiple_of(peer * d, d), d)
            part = raw[clip, 4, :, lanes]
            qsend[clip, peer, :, :d] = (part.astype(WIDE) * live[clip]).astype(NARROW)
            qsend[clip, peer, :, d:] = raw[clip, 5, :, lanes]

            @pl.when(slot != own_slot)
            def _():
                pltpu.make_async_remote_copy(
                    src_ref=qsend.at[clip, peer],
                    dst_ref=qbuf.at[clip, pl.ds(pl.multiple_of(slot * tok, tok), tok)],
                    send_sem=q_ss.at[clip],
                    recv_sem=q_rs.at[clip, slot // GROUP],
                    device_id=device(peer, my_f),
                ).start()

            return carry

        lax.fori_loop(0, n_seq, one, 0)
        qbuf[clip, own_rows] = qsend[clip, me]

    def drain(ref, sem):
        pltpu.make_async_copy(ref, ref, sem).wait()

    pl.semaphore_wait(barrier, n_seq - 1 + len(x_peers) + len(y_far))

    def to_neighbour(sign, part, step):
        pltpu.make_async_remote_copy(
            src_ref=part, dst_ref=part, send_sem=w_ss.at[0], recv_sem=w_rs.at[0, step],
            device_id=device(ring_z(1, sign) * GROUP + y_lo * CORE + core, my_f),
        ).start()

    def relay(far):
        for side, sign in ((2 * far - 1, 1), (2 * far, -1)):
            part = wbuf.at[ring_z(side, -1), y_lo, core, y_hi, x]
            drain(part, w_rs.at[0, side])
            if 2 * far + 2 < n_z:
                to_neighbour(sign, part, side + 2)
            else:
                half = part.shape[1] // 2
                lanes = slice(0, half) if sign == 1 else slice(half, 2 * half)
                to_neighbour(sign, part.at[:, lanes], 2 * far + 1)

    def spread_y(step):
        part = wbuf.at[ring_z(step, -1), y_lo, core, y_hi, x]
        for peer in y_peers:
            pltpu.make_async_remote_copy(
                src_ref=part, dst_ref=part, send_sem=w_ss.at[1], recv_sem=w_rs.at[1, step],
                device_id=peer,
            ).start()

    def spread_x(step):
        drain(wbuf.at[0, 0, 0, 0, : len(y_peers)], w_rs.at[1, step])
        part = wbuf.at[ring_z(step, -1), :, core, :, x]
        for peer in x_peers:
            pltpu.make_async_remote_copy(
                src_ref=part, dst_ref=part, send_sem=w_ss.at[2], recv_sem=w_rs.at[2, step],
                device_id=peer,
            ).start()

    def spread_core(step, carry):
        drain(wbuf.at[0, :, 0, :, : n_x - 1], w_rs.at[2, step])
        part = wbuf.at[ring_z(step, -1), :, core]
        pltpu.make_async_remote_copy(
            src_ref=part, dst_ref=part, send_sem=w_ss.at[3], recv_sem=w_rs.at[3, step],
            device_id=device(z * GROUP + y_lo * CORE + (core + 1) % CORE, my_f),
        ).start()
        return carry

    own_weight.wait()
    mine = wbuf.at[z, y_lo, core, y_hi, x]
    to_neighbour(1, mine, 1)
    to_neighbour(-1, mine, 2)
    spread_y(0)
    await_kv(0)
    hops = n_z // 2
    send_kv(0, 0, GROUP)
    for far in range(1, hops):
        relay(far)
        spread_y(2 * far - 1)
        spread_y(2 * far)
        for step in range(max(2 * far - 5, 0), 2 * far - 3):
            spread_x(step)
        send_kv(0, (2 * far - 1) * GROUP, (2 * far + 1) * GROUP)
    send_kv(0, (n_z - 1) * GROUP, n_seq)
    drain(wbuf.at[0, 0, 0, 0, 0], w_rs.at[0, n_z - 1])
    spread_y(n_z - 1)
    send_q(0)

    def continue_x(step, carry):
        spread_x(step)
        return carry

    lax.fori_loop(n_z - 5, n_z, continue_x, 0)
    await_kv(1)
    send_kv(1, 0, n_seq)
    send_q(1)
    for copy in late_loads:
        copy.start()

    scale = d ** (-0.5)
    to_exponent = scale * math.log2(math.e)
    step_rows = 16

    def give_back(clip, index):
        for part in range(GROUP):
            slot = index * GROUP + part
            copy = pltpu.make_async_remote_copy(
                src_ref=osend.at[clip, slot],
                dst_ref=orecv.at[clip, me],
                send_sem=o_ss.at[clip],
                recv_sem=o_rs.at[clip, index],
                device_id=device(seq_peer(slot, -1), my_f),
            )
            if part:
                copy.start()
            else:
                pl.when(index != n_z - 1)(copy.start)

    def attend(clip):
        drain(kvbuf.at[clip, tok:], kv_rs.at[clip])

        def block(index, carry):
            start = pl.multiple_of(index * rows, rows)

            @pl.when(index == n_z - 1)
            def _():
                drain(qbuf.at[clip, tok:rows], q_rs.at[clip, index])

            @pl.when(index != n_z - 1)
            def _():
                drain(qbuf.at[clip, :rows], q_rs.at[clip, index])

            if clip:
                give_back(clip - 1, index)
            both = qbuf[clip, pl.ds(start, rows)]
            plain = both[:, d:]
            left = jnp.concatenate(
                [jnp.concatenate([plain, jnp.zeros_like(plain)], 1), both], 0
            )
            scores[...] = lax.dot_general(
                left, kvbuf[clip, :, : 2 * d], (((1,), (1,)), ((), ())),
                preferred_element_type=WIDE,
            )

            def soften(step, carry):
                at = pl.multiple_of(step * step_rows, step_rows)
                exponent = scores[pl.ds(at, step_rows)] * to_exponent
                weight = jnp.exp2(exponent - jnp.max(exponent, 1, keepdims=True))
                norm = jnp.sum(weight, 1, keepdims=True)
                slant = scores[pl.ds(rows + at, step_rows)]
                centre = jnp.sum(weight * slant, 1, keepdims=True) / norm
                probs[pl.ds(at, step_rows)] = weight.astype(NARROW)
                probs[pl.ds(rows + at, step_rows)] = (weight * (slant - centre)).astype(NARROW)
                sums[pl.ds(at, step_rows)] = jnp.broadcast_to(1.0 / norm, (step_rows, d))
                return carry

            lax.fori_loop(0, rows // step_rows, soften, 0, unroll=4)
            result = jnp.dot(
                probs[...], kvbuf[clip, :, 2 * d :], preferred_element_type=WIDE
            )
            inverse = sums[...]
            value = (result[:rows, :d] * inverse).astype(NARROW)
            value_tan = (
                (result[rows:, :d] * scale + result[:rows, d:]) * inverse
            ).astype(NARROW)
            for part in range(GROUP):
                slot = index * GROUP + part
                at = slice(part * tok, (part + 1) * tok)
                osend[clip, slot, :tok] = value[at]
                osend[clip, slot, tok:] = value_tan[at]
            if clip == CLIPS - 1:
                give_back(clip, index)
            return carry

        lax.fori_loop(0, n_z, block, 0)
        orecv[clip, me] = osend[clip, own_slot]

    attend(0)
    lax.fori_loop(0, EARLY_CHUNKS, spread_core, 0)
    attend(1)
    lax.fori_loop(EARLY_CHUNKS, n_z, spread_core, 0)

    def settle(step, carry):
        drain(wbuf.at[0, :, 0], w_rs.at[3, step])
        return carry

    lax.fori_loop(0, n_z, settle, 0)
    for copy in late_loads:
        copy.wait()

    tile = 512
    depth = GROUP * d
    steps = gatebuf.shape[1]

    picked = [
        (lax.broadcasted_iota(jnp.int32, (steps, 1), 0) == time_ref[clip]).astype(WIDE)
        for clip in range(CLIPS)
    ]

    def gather(step):
        at = ring_z(n_z - 1 - step, 1)
        for clip in range(CLIPS):
            for part in range(GROUP):
                joined[clip * 2 * tok : (clip + 1) * 2 * tok, part * d : (part + 1) * d] = orecv[
                    clip, at * GROUP + part
                ]
        return at

    def product(at, index):
        lanes = pl.ds(pl.multiple_of(index * tile, tile), tile)
        weight = wbuf[at, :, :, :, :, :, lanes].reshape(depth, tile)
        return lanes, jnp.dot(joined[...], weight, preferred_element_type=WIDE)

    def project(step, carry):
        for clip in range(CLIPS):
            drain(orecv.at[clip, :GROUP], o_rs.at[clip, step])
        at = gather(step)

        def one(index, carry):
            lanes, both = product(at, index)

            @pl.when(step == 0)
            def _():
                total[:, lanes] = both

            @pl.when(step != 0)
            def _():
                total[:, lanes] += both

            return carry

        lax.fori_loop(0, n_out // tile, one, 0, unroll=True)
        return carry

    lax.fori_loop(0, n_z - 1, project, 0)
    for clip in range(CLIPS):
        drain(orecv.at[clip, : GROUP - 1], o_rs.at[clip, n_z - 1])
    nearest = gather(n_z - 1)

    def store(which, lanes):
        return pltpu.make_async_copy(
            outbuf.at[which, :, :, lanes], (out_ref, tan_ref)[which].at[:, :, lanes],
            store_sem.at[which],
        )

    def finish(index, carry):
        lanes, both = product(nearest, index)
        both = total[:, lanes] + both
        for clip in range(CLIPS):
            gate = jnp.sum(gatebuf[0, :, lanes] * picked[clip], 0, keepdims=True)
            slope = jnp.sum(gatebuf[1, :, lanes] * picked[clip], 0, keepdims=True)
            at = clip * 2 * tok
            plain, tangent = both[at : at + tok], both[at + tok : at + 2 * tok]
            outbuf[0, clip, :, lanes] = (
                resbuf[0, clip, :, lanes].astype(WIDE) + gate * plain
            ).astype(NARROW)
            outbuf[1, clip, :, lanes] = (
                resbuf[1, clip, :, lanes].astype(WIDE) * live[clip] + slope * plain + gate * tangent
            ).astype(NARROW)
        for which in range(2):
            store(which, lanes).start()
        return carry

    lax.fori_loop(0, n_out // tile, finish, 0, unroll=True)
    for which in range(2):
        drain(outbuf.at[which], store_sem.at[which])

    for clip in range(CLIPS):
        drain(kvsend.at[clip, : n_seq - 1], kv_ss.at[clip])
        drain(qsend.at[clip, : n_seq - 1], q_ss.at[clip])
        drain(osend.at[clip, : n_seq - 1], o_ss.at[clip])
    drain(wbuf.at[: n_z - 1, 0, 0, 0, 0], w_ss.at[0])
    drain(wbuf.at[:, 0, 0, 0, : len(y_peers)], w_ss.at[1])
    drain(wbuf.at[:, :, 0, :, : n_x - 1], w_ss.at[2])
    drain(wbuf.at[:, :, 0], w_ss.at[3])


def dims_y_hi(dims):
    return Y_HI


def body(*args):
    (queries, key_rows, value_rows, query_tan, key_tan, value_tan, residual, residual_tan,
     cond_mask, time_index, gate_table, gate_slope, out_weight) = args
    clips, tok, width = queries.shape
    n_out = out_weight.shape[1]
    n_seq = lax.axis_size("seq")
    n_z = n_seq // GROUP
    n_x = lax.axis_size("fsdp") // Y_HI
    d = HEAD_DIM
    length = n_seq * tok
    rows = GROUP * tok
    steps = gate_table.shape[0]
    w_rows = out_weight.shape[0]
    anywhere = pl.BlockSpec(memory_space=pl.ANY)
    vmem = pl.BlockSpec(memory_space=pltpu.VMEM)
    smem = pl.BlockSpec(memory_space=pltpu.SMEM)
    out_shape = jax.ShapeDtypeStruct((clips, tok, n_out), NARROW)
    dma = pltpu.SemaphoreType.DMA
    return pl.pallas_call(
        functools.partial(kernel, (n_z, n_x, tok, n_out)),
        out_shape=(out_shape, out_shape),
        in_specs=[anywhere] * 8 + [vmem, smem] + [anywhere] * 3,
        out_specs=(anywhere, anywhere),
        scratch_shapes=[
            pltpu.VMEM((clips, 6, tok, width), NARROW),
            pltpu.VMEM((clips, n_seq, tok, 4 * d), NARROW),
            pltpu.VMEM((clips, length, 4 * d), NARROW),
            pltpu.VMEM((clips, n_seq, tok, 2 * d), NARROW),
            pltpu.VMEM((clips, length, 2 * d), NARROW),
            pltpu.VMEM((clips, n_seq, 2 * tok, d), NARROW),
            pltpu.VMEM((clips, n_seq, 2 * tok, d), NARROW),
            pltpu.VMEM((n_z, Y_LO, CORE, Y_HI, n_x, w_rows, n_out), NARROW),
            pltpu.VMEM((2, clips, tok, n_out), NARROW),
            pltpu.VMEM((2, steps, n_out), WIDE),
            pltpu.VMEM((2 * rows, length), WIDE),
            pltpu.VMEM((2 * rows, length), NARROW),
            pltpu.VMEM((rows, d), WIDE),
            pltpu.VMEM((clips * 2 * tok, GROUP * d), NARROW),
            pltpu.VMEM((clips * 2 * tok, n_out), WIDE),
            pltpu.VMEM((2, clips, tok, n_out), NARROW),
            dma((clips, 6)), dma((4,)),
            dma((clips,)), dma((clips,)), dma((clips,)), dma((clips, n_z)), dma((clips,)), dma((clips, n_z)),
            dma((4,)), dma((4, n_z)), dma((1,)), dma((2,)),
        ],
        compiler_params=pltpu.CompilerParams(
            collective_id=0, has_side_effects=True, vmem_limit_bytes=62 * 2**20
        ),
        cost_estimate=pl.CostEstimate(
            flops=20 * 10**9, bytes_accessed=12 * 2**20, transcendentals=8 * 2**20
        ),
    )(*args)


def solution(mesh):
    tokens = P("fsdp", "seq", None)
    in_specs = (tokens,) * 8 + (P("fsdp", "seq"), P("fsdp"), P(), P(), P(("seq", "fsdp"), None))
    return jax.shard_map(
        body, mesh=mesh, in_specs=in_specs, out_specs=(tokens, tokens), check_vma=False
    )
```
